512 devices in a mesh: seq: 64 (over y, z), head: 8 (over x, core).
Axes of the slice: x: 4, y: 8, z: 8, core: 2. Of those that a mesh axis runs over, the one named last changes fastest.
Arguments:
- queries: bfloat16 [16384, 4096], P('seq', 'head'), may hold values from -120 to 120
- noisy_keys: bfloat16 [16384, 4096], P('seq', 'head'), may hold values from -120 to 120
- noisy_values: bfloat16 [16384, 4096], P('seq', 'head'), may hold values from -6 to 6
- clean_keys: bfloat16 [16384, 4096], P('seq', 'head'), may hold values from -120 to 120
- clean_values: bfloat16 [16384, 4096], P('seq', 'head'), may hold values from -6 to 6
- query_gain: float32 [4096], P('head'), may hold values from 0.25 to 1.75
- key_gain: float32 [4096], P('head'), may hold values from 0.25 to 1.75
- first_block: int32 [512], P('seq'), may hold values from 0 to 511, as said below
- loss_mask: int32 [16384], P('seq'), may hold values 0 or 1
- grad_output: bfloat16 [16384, 4096], P('seq', 'head'), may hold values from -6 to 6
Outputs:
- attended: bfloat16 [16384, 4096], P('seq', 'head')
- grad_queries: bfloat16 [16384, 4096], P('seq', 'head')
- grad_noisy_keys: bfloat16 [16384, 4096], P('seq', 'head')
- grad_noisy_values: bfloat16 [16384, 4096], P('seq', 'head')
- grad_clean_keys: bfloat16 [16384, 4096], P('seq', 'head')
- grad_clean_values: bfloat16 [16384, 4096], P('seq', 'head')
The draws below stay inside these ranges and needn't reach their ends.
Inputs may be any that keep to these rules, and one draw needn't show every extreme that they name: first_block[b] is the first block of the document holding block b: it never falls, first_block[first_block[b]] = first_block[b], and b - first_block[b] < 48; at least one document holds exactly 48 blocks, and the last block is a document of its own.
All inputs are finite; a program needn't handle non-finite values. No bound on the sum of `loss_mask` on one device may be relied on, other than what follows from the above.
Results may differ from the reference program's by a relative error of at most 0.01055.
The reference program's roundings to bfloat16 on the way count: a program that leaves them out, or rounds other values in their place, can miss the bound.
Values may be sent and summed in bfloat16 or wider, within the bound.
No kernel may reach another device: no remote copies, remote signals or barrier semaphores. Data moves between devices by JAX's collectives and lax.ppermute only.
A program may use at most 64 MiB of HBM per device.

```python
import math
import jax
import jax.numpy as jnp
from jax import lax

HEAD_DIM = 128
BLOCK = 32
REACH = 6
TOK_DEV = 256
HEADS = 32
WIDTH = 4096
TOKENS = 16384
NBLK = 512
DOC_BLOCKS = 48


def spread_rows(key, base, ramp, row_top):
    key_column, key_row = jax.random.split(key)
    fraction = jnp.arange(WIDTH, dtype=jnp.float32) / WIDTH
    column = jnp.sqrt(ramp) ** fraction * jnp.exp(jax.random.uniform(key_column, (WIDTH,)) * math.log(10.0))
    row_scale = jnp.exp(jax.random.uniform(key_row, (TOKENS, 1)) * math.log(row_top))
    return jnp.clip(0.1 * base * column[None, :] * row_scale, -120.0, 120.0)


def draw_queries(key, part):
    key_base, key_scale = jax.random.split(jax.random.fold_in(key, 1))
    base = jax.random.normal(key_base, (TOKENS, WIDTH))
    return spread_rows(key_scale, base, 3.0, 10.0).astype(jnp.bfloat16)


def draw_noisy_keys(key, part):
    key_base, key_scale = jax.random.split(jax.random.fold_in(key, 2))
    base = jax.random.normal(key_base, (TOKENS, WIDTH))
    return spread_rows(key_scale, base, 3.0, 10.0).astype(jnp.bfloat16)


def draw_clean_keys(key, part):
    key = jax.random.fold_in(key, 3)
    key_base, key_scale = jax.random.split(key)
    base = jax.random.normal(key_base, (TOKENS, WIDTH))
    return spread_rows(key_scale, base, 3.0, 10.0).astype(jnp.bfloat16)


def draw_first_block(key, part):
    key = jax.random.fold_in(key, 11)
    key_lengths, key_lead = jax.random.split(key)
    lengths = jax.random.randint(key_lengths, (NBLK,), 1, DOC_BLOCKS + 1)
    lead = jax.random.randint(key_lead, (), 1, TOK_DEV // BLOCK)
    lengths = lengths.at[0].set(lead).at[1].set(DOC_BLOCKS)
    starts = jnp.cumsum(lengths) - lengths
    index = jnp.arange(NBLK)
    document = jnp.sum((starts[None, :] <= index[:, None]).astype(jnp.int32), axis=1) - 1
    firsts = jnp.take(starts, document).astype(jnp.int32)
    return firsts.at[NBLK - 1].set(NBLK - 1)


def place_ends(array, stream_key, smallest, top_value):
    longest = array.shape.index(max(array.shape))
    spots = []
    for shift in (0, 1):
        where = [jax.random.randint(jax.random.fold_in(stream_key, axis), (), 0, length) for axis, length in enumerate(array.shape)]
        where[longest] = (where[longest] + shift) % array.shape[longest]
        spots.append(tuple(where))
    return array.at[spots[0]].set(smallest).at[spots[1]].set(top_value)


def levels(stream_key, dims, cuts, smallest, high):
    loudness, own = 1.0, jax.random.fold_in(stream_key, 6)
    for dim, blocks in cuts:
        steps = jnp.exp(jax.random.uniform(jax.random.fold_in(own, dim), (blocks,), jnp.float32, smallest / len(cuts), high / len(cuts)))
        loudness = loudness * jnp.repeat(steps, dims[dim] // blocks).reshape([-1 if axis == dim else 1 for axis in range(len(dims))])
    return loudness


def normal_values(stream_key, dims, width, bound, pieces=(), kind=jnp.bfloat16):
    level = levels(stream_key, dims, pieces, -0.22, 0.18) if pieces else 1.0
    drawn = jax.random.normal(stream_key, dims, jnp.float32) * width * level
    return jnp.minimum(jnp.maximum(drawn, -bound), bound).astype(kind)


def setup_inputs(seed: int = 0) -> dict:
    seeds = jax.random.split(jax.random.key(seed), 11)
    return {
        "queries": draw_queries(jax.random.fold_in(seeds[10], 71), 0),
        "noisy_keys": draw_noisy_keys(jax.random.fold_in(seeds[10], 71), 0),
        "noisy_values": normal_values(seeds[2], (TOKENS, WIDTH), 1.0, 6.0, ((0, 64), (1, 8))),
        "clean_keys": draw_clean_keys(jax.random.fold_in(seeds[10], 71), 0),
        "clean_values": normal_values(seeds[4], (TOKENS, WIDTH), 1.0, 6.0, ((0, 64), (1, 8))),
        "query_gain": jnp.clip(1.0 + 0.15 * jax.random.normal(seeds[5], (WIDTH,), jnp.float32), 0.25, 1.75),
        "key_gain": jnp.clip(1.0 + 0.15 * jax.random.normal(seeds[6], (WIDTH,), jnp.float32), 0.25, 1.75),
        "first_block": draw_first_block(jax.random.fold_in(seeds[10], 71), 0),
        "loss_mask": place_ends((jax.random.randint(seeds[8], (TOKENS,), 0, 2) < 1).astype(jnp.int32), jax.random.fold_in(seeds[8], 1), 0, 1),
        "grad_output": normal_values(seeds[9], (TOKENS, WIDTH), 1.0, 6.0, ((0, 64), (1, 8))),
    }


EPS = 1e-06

def unit_rows(raw, gain):
    values = raw.astype(jnp.float32)
    inverse = lax.rsqrt(lax.optimization_barrier(jnp.sum(values * values, axis=1)) / WIDTH + EPS)
    unit = (values * inverse[:, None] * gain[None, :]).astype(jnp.bfloat16)
    return (values, inverse, unit)

def unit_backward(values, inverse, gain, grad_unit):
    term = gain[None, :] * grad_unit
    inner = lax.optimization_barrier(jnp.sum(term * values, axis=1))
    return (inverse[:, None] * term - values * (inverse ** 3 * inner / WIDTH)[:, None]).astype(jnp.bfloat16)

def rounded(weights):
    narrow = lax.optimization_barrier(weights.astype(jnp.bfloat16))
    return narrow.astype(jnp.float32)

def reference(queries, noisy_keys, noisy_values, clean_keys, clean_values, query_gain, key_gain, first_block, loss_mask, grad_output):
    softmax_scale = HEAD_DIM ** (-0.5)
    window = (REACH + 1) * TOK_DEV
    margin = REACH * TOK_DEV
    groups = TOKENS // TOK_DEV
    heads_shape = (TOKENS, HEADS, HEAD_DIM)
    query_raw, query_inverse, query_unit = unit_rows(queries, query_gain)
    noisy_raw, noisy_inverse, noisy_unit = unit_rows(noisy_keys, key_gain)
    clean_raw, clean_inverse, clean_unit = unit_rows(clean_keys, key_gain)
    query_heads = query_unit.reshape(heads_shape).astype(jnp.float32)
    noisy_heads = noisy_unit.reshape(heads_shape).astype(jnp.float32)
    clean_heads = clean_unit.reshape(heads_shape).astype(jnp.float32)
    noisy_value_heads = noisy_values.reshape(heads_shape).astype(jnp.float32)
    clean_value_heads = clean_values.reshape(heads_shape).astype(jnp.float32)
    grad_masked = grad_output * loss_mask[:, None].astype(jnp.bfloat16)
    grad_heads = grad_masked.reshape(heads_shape).astype(jnp.float32)
    token_block = jnp.arange(TOKENS, dtype=jnp.int32) // BLOCK
    token_first = jnp.take(first_block, token_block)
    zero_heads = jnp.zeros((margin, HEADS, HEAD_DIM), jnp.float32)
    clean_pad = jnp.concatenate([zero_heads, clean_heads], axis=0)
    clean_value_pad = jnp.concatenate([zero_heads, clean_value_heads], axis=0)
    block_pad = jnp.concatenate([jnp.full((margin,), -1, jnp.int32), token_block])

    def query_group(index):
        start = (index * TOK_DEV).astype(jnp.int32)
        query_part = lax.dynamic_slice_in_dim(query_heads, start, TOK_DEV, 0)
        noisy_part = lax.dynamic_slice_in_dim(noisy_heads, start, TOK_DEV, 0)
        noisy_value_part = lax.dynamic_slice_in_dim(noisy_value_heads, start, TOK_DEV, 0)
        grad_part = lax.dynamic_slice_in_dim(grad_heads, start, TOK_DEV, 0)
        query_block = lax.dynamic_slice_in_dim(token_block, start, TOK_DEV, 0)
        query_first = lax.dynamic_slice_in_dim(token_first, start, TOK_DEV, 0)
        clean_part = lax.dynamic_slice_in_dim(clean_pad, start, window, 0)
        clean_value_part = lax.dynamic_slice_in_dim(clean_value_pad, start, window, 0)
        clean_block = lax.dynamic_slice_in_dim(block_pad, start, window, 0)
        own_seen = query_block[:, None] == query_block[None, :]
        clean_seen = (clean_block[None, :] < query_block[:, None]) & (clean_block[None, :] >= query_first[:, None])
        seen = jnp.concatenate([own_seen, clean_seen], axis=1)
        key_all = jnp.concatenate([noisy_part, clean_part], axis=0)
        value_all = jnp.concatenate([noisy_value_part, clean_value_part], axis=0)
        scores = jnp.einsum('ihd,jhd->hij', query_part, key_all) * softmax_scale
        masked = jnp.where(seen[None], scores, -jnp.inf)
        top = lax.optimization_barrier(jnp.max(masked, axis=2))
        lse = top + jnp.log(lax.optimization_barrier(jnp.sum(jnp.exp(masked - top[:, :, None]), axis=2)))
        weights = jnp.exp(masked - lse[:, :, None])
        weight_bf = rounded(weights)
        output = jnp.einsum('hij,jhd->ihd', weight_bf, value_all).astype(jnp.bfloat16)
        delta = lax.optimization_barrier(jnp.sum(grad_part * output.astype(jnp.float32), axis=2))
        dweights = jnp.einsum('ihd,jhd->hij', grad_part, value_all)
        dscores = rounded(weights * (dweights - delta.T[:, :, None]))
        grad_query = jnp.einsum('hij,jhd->ihd', dscores, key_all) * softmax_scale
        grad_noisy = jnp.einsum('hij,ihd->jhd', dscores[:, :, :TOK_DEV], query_part) * softmax_scale
        grad_noisy_value = jnp.einsum('hij,ihd->jhd', weight_bf[:, :, :TOK_DEV], grad_part)
        return (output, grad_query, grad_noisy, grad_noisy_value, lse.T, delta)
    group_index = jnp.arange(groups, dtype=jnp.int32)
    output, grad_query, grad_noisy, grad_noisy_value, lse_all, delta_all = lax.map(query_group, group_index)
    attended = output.reshape(TOKENS, WIDTH)
    lse_all = lse_all.reshape(TOKENS, HEADS)
    delta_all = delta_all.reshape(TOKENS, HEADS)
    zero_rows = jnp.zeros((margin, HEADS), jnp.float32)
    query_tail = jnp.concatenate([query_heads, zero_heads], axis=0)
    grad_tail = jnp.concatenate([grad_heads, zero_heads], axis=0)
    lse_tail = jnp.concatenate([lse_all, zero_rows], axis=0)
    delta_tail = jnp.concatenate([delta_all, zero_rows], axis=0)
    block_tail = jnp.concatenate([token_block, jnp.full((margin,), NBLK, jnp.int32)])
    first_tail = jnp.concatenate([token_first, jnp.full((margin,), NBLK, jnp.int32)])
    split_shape = (REACH + 1, TOK_DEV, HEADS, HEAD_DIM)

    def key_group(index):
        start = (index * TOK_DEV).astype(jnp.int32)
        key_part = lax.dynamic_slice_in_dim(clean_heads, start, TOK_DEV, 0)
        value_part = lax.dynamic_slice_in_dim(clean_value_heads, start, TOK_DEV, 0)
        key_block = lax.dynamic_slice_in_dim(token_block, start, TOK_DEV, 0)
        query_part = lax.dynamic_slice_in_dim(query_tail, start, window, 0)
        grad_part = lax.dynamic_slice_in_dim(grad_tail, start, window, 0)
        lse_part = lax.dynamic_slice_in_dim(lse_tail, start, window, 0)
        delta_part = lax.dynamic_slice_in_dim(delta_tail, start, window, 0)
        query_block = lax.dynamic_slice_in_dim(block_tail, start, window, 0)
        query_first = lax.dynamic_slice_in_dim(first_tail, start, window, 0)
        seen = (key_block[None, :] < query_block[:, None]) & (key_block[None, :] >= query_first[:, None])
        scores = jnp.einsum('ihd,jhd->hij', query_part, key_part) * softmax_scale
        weights = jnp.where(seen[None], jnp.exp(scores - lse_part.T[:, :, None]), 0.0)
        weight_bf = rounded(weights)
        dweights = jnp.einsum('ihd,jhd->hij', grad_part, value_part)
        dscores = rounded(weights * (dweights - delta_part.T[:, :, None]))
        score_split = dscores.reshape(HEADS, REACH + 1, TOK_DEV, TOK_DEV)
        weight_split = weight_bf.reshape(HEADS, REACH + 1, TOK_DEV, TOK_DEV)
        query_split = query_part.reshape(split_shape)
        grad_split = grad_part.reshape(split_shape)
        key_parts = rounded(jnp.einsum('hnij,nihd->njhd', score_split, query_split))
        value_parts = rounded(jnp.einsum('hnij,nihd->njhd', weight_split, grad_split))
        grad_key = lax.optimization_barrier(jnp.sum(key_parts, axis=0)) * softmax_scale
        grad_value = lax.optimization_barrier(jnp.sum(value_parts, axis=0))
        return (grad_key, grad_value)
    grad_clean, grad_clean_value = lax.map(key_group, group_index)
    grad_queries = unit_backward(query_raw, query_inverse, query_gain, grad_query.reshape(TOKENS, WIDTH))
    grad_noisy_keys = unit_backward(noisy_raw, noisy_inverse, key_gain, grad_noisy.reshape(TOKENS, WIDTH))
    grad_clean_keys = unit_backward(clean_raw, clean_inverse, key_gain, grad_clean.reshape(TOKENS, WIDTH))
    grad_noisy_values = grad_noisy_value.reshape(TOKENS, WIDTH).astype(jnp.bfloat16)
    grad_clean_values = grad_clean_value.reshape(TOKENS, WIDTH).astype(jnp.bfloat16)
    return (attended, grad_queries, grad_noisy_keys, grad_noisy_values, grad_clean_keys, grad_clean_values)
```

```python
from functools import partial

import jax
import jax.numpy as jnp
from jax import lax
from jax.experimental import pallas as pl
from jax.experimental.pallas import tpu as pltpu
from jax.sharding import PartitionSpec as P

HEAD_DIM = 128
BLOCK = 32
RING = 8
EPS = 1e-06
LOG2E = 1.4426950408889634
HIDDEN = -1e30
SCALE = HEAD_DIM ** (-0.5)
F32 = jnp.float32
BF16 = jnp.bfloat16

OWN, FOURTH = (0, 0), (4, -4)
FIRST = [(1, -1), (-1, 1)]
SECOND = [(2, -2), (-2, 2)]
THIRD = [(3, -3), (-3, 3)]
NOISY = None


def shifted(shard, by):
    count = lax.axis_size("seq")
    return lax.ppermute(shard, "seq", [(i, (i + by) % count) for i in range(count)])


def ring_groups():
    count = lax.axis_size("seq")
    return [list(range(start, start + RING)) for start in range(0, count, RING)]


def ring_gather(shard):
    return lax.all_gather(shard, "seq", axis_index_groups=ring_groups(), tiled=True)


def ring_scatter(parts):
    return lax.psum_scatter(
        parts, "seq", scatter_dimension=0, axis_index_groups=ring_groups(), tiled=True
    )


def swapped(shard, first):
    pairs = []
    for start in range(0, lax.axis_size("seq"), RING):
        for left in range(first, RING, 2):
            one, other = start + left, start + (left + 1) % RING
            pairs += [(one, other), (other, one)]
    return lax.ppermute(shard, "seq", pairs)


def add_kernel(unread, *refs):
    left_ref, right_ref, out_ref = refs[unread:]
    out_ref[...] = left_ref[...] + right_ref[...]


def head_sum(values, before_last=()):
    count = lax.axis_size("head")
    if count & (count - 1):
        return lax.psum(values, "head")
    bit = 1
    while bit < count:
        other = lax.ppermute(values, "head", [(i, i ^ bit) for i in range(count)])
        if before_last and 4 * bit == count:
            (values,) = call(
                partial(add_kernel, len(before_last)),
                "add",
                [(values.shape, F32)],
                1024,
                values,
                other,
                unread=before_last,
            )
        else:
            values = values + other
        bit *= 2
    return values


def dot(left, right):
    return jnp.dot(left, right, preferred_element_type=F32)


def lanes(head):
    return slice(head * HEAD_DIM, (head + 1) * HEAD_DIM)


def stacked(blocks):
    return jnp.concatenate(blocks, axis=0)


def tile_place(where_ref, tile):
    if tile is NOISY:
        return RING, 0
    place = where_ref[0]
    far = jnp.where(where_ref[1] == 1, tile[1], tile[0])
    index = lax.rem(place + far + RING, RING)
    return index, jnp.where(index > place, 1, 0)


def value_rows(index, rows):
    return pl.ds(pl.multiple_of(index * rows, rows), rows)


def softmax_tile(keys, values, query_t, shift):
    raw = dot(keys, query_t) * (SCALE * LOG2E)
    scores = [
        raw[block * BLOCK : (block + 1) * BLOCK] + shift[block : block + 1]
        for block in range(shift.shape[0])
    ]
    top = scores[0]
    for block in scores[1:]:
        top = jnp.maximum(top, block)
    top = jnp.max(top, axis=0, keepdims=True)
    weights = [jnp.exp2(block - top) for block in scores]
    total = weights[0]
    for block in weights[1:]:
        total = total + block
    total = jnp.sum(total, axis=0, keepdims=True)
    acc = dot(values.T, stacked([w.astype(BF16) for w in weights]))
    return top, total, acc


def forward_kernel(
    tiles,
    where_ref,
    bias_ref,
    q_ref,
    q_next_ref,
    g_ref,
    g_next_ref,
    noisy_values_ref,
    values_ref,
    *refs,
):
    count = len(tiles)
    keys_refs = refs[:count]
    qt_ref, gt_ref, q_both, g_both, stat_ref, acc_ref = refs[count:]
    rows = bias_ref.shape[-1]
    heads = q_ref.shape[1] // HEAD_DIM
    for which, (q, g) in enumerate(((q_ref, g_ref), (q_next_ref, g_next_ref))):
        q_both[which], g_both[which] = q[...], g[...]
        for head in range(heads):
            part = lanes(head)
            qt_ref[which, part, :] = q[:, part].T
            gt_ref[which, part, :] = g[:, part].T
    for number, tile in enumerate(tiles):
        index, which = tile_place(where_ref, tile)
        for head in range(heads):
            part = lanes(head)
            if tile is NOISY:
                values = noisy_values_ref[:, part]
            else:
                values = values_ref[value_rows(index, rows), part]
            top, total, acc = softmax_tile(
                keys_refs[number][:, part], values, qt_ref[which, part, :], bias_ref[index]
            )
            stat_ref[2 * number, head : head + 1, :] = top
            stat_ref[2 * number + 1, head : head + 1, :] = total
            acc_ref[number, part, :] = acc


def forward_end_kernel(
    tiles, before, where_ref, bias_ref, qt_ref, gt_ref, stat_ref, acc_ref, values_ref, *refs
):
    count = len(tiles)
    keys_refs = refs[:count]
    own_stat, next_stat, own_acc, next_acc = refs[count:]
    rows = bias_ref.shape[-1]
    heads = values_ref.shape[1] // HEAD_DIM
    places = [tile_place(where_ref, tile) for tile in (*before, *tiles)]
    for head in range(heads):
        part = lanes(head)
        parts = [
            (
                stat_ref[2 * number, head : head + 1, :],
                stat_ref[2 * number + 1, head : head + 1, :],
                acc_ref[number, part, :],
            )
            for number in range(len(before))
        ]
        for number, tile in enumerate(tiles):
            index, which = places[len(before) + number]
            parts.append(
                softmax_tile(
                    keys_refs[number][:, part],
                    values_ref[value_rows(index, rows), part],
                    qt_ref[which, part, :],
                    bias_ref[index],
                )
            )
        for which, (stat, out) in enumerate(((own_stat, own_acc), (next_stat, next_acc))):
            tops = [
                jnp.where(place[1] == which, one[0], HIDDEN)
                for place, one in zip(places, parts)
            ]
            top = tops[0]
            for one in tops[1:]:
                top = jnp.maximum(top, one)
            total, acc = 0.0, 0.0
            for place, one in zip(places, parts):
                fade = jnp.where(place[1] == which, jnp.exp2(one[0] - top), 0.0)
                total = total + fade * one[1]
                acc = acc + fade * one[2]
            stat[head : head + 1, :] = top
            stat[heads + head : heads + head + 1, :] = total
            stat[2 * heads + head : 2 * heads + head + 1, :] = jnp.sum(
                gt_ref[which, part, :].astype(F32) * acc, axis=0, keepdims=True
            )
            out[part, :] = acc.astype(out.dtype)


def merged(first, second, heads):
    top = jnp.maximum(first[:heads], second[:heads])
    fades = [jnp.exp2(s[:heads] - top) for s in (first, second)]
    total = fades[0] * first[heads : 2 * heads] + fades[1] * second[heads : 2 * heads]
    inverse = 1.0 / total
    fades = [fade * inverse for fade in fades]
    delta = fades[0] * first[2 * heads : 3 * heads] + fades[1] * second[2 * heads : 3 * heads]
    return stacked([top + jnp.log2(total), delta, *fades])


def value_grad_kernel(
    tiles,
    where_ref,
    bias_ref,
    own_stat,
    next_stat,
    before_stat,
    after_stat,
    qt_ref,
    g_both,
    *refs,
):
    keys_refs = refs[: len(tiles)]
    final_ref, dv_ref = refs[len(tiles) :]
    rows = bias_ref.shape[-1]
    heads = dv_ref.shape[1] // HEAD_DIM
    final_ref[0] = merged(own_stat[...], before_stat[...], heads)
    final_ref[1] = merged(next_stat[...], after_stat[...], heads)
    for number, tile in enumerate(tiles):
        index, which = tile_place(where_ref, tile)
        for head in range(heads):
            part = lanes(head)
            raw = dot(keys_refs[number][:, part], qt_ref[which, part, :]) * (SCALE * LOG2E)
            shift = bias_ref[index] - final_ref[which, head : head + 1, :]
            weight = stacked(
                [
                    jnp.exp2(
                        raw[block * BLOCK : (block + 1) * BLOCK] + shift[block : block + 1]
                    ).astype(BF16)
                    for block in range(rows // BLOCK)
                ]
            )
            dv_ref[value_rows(index, rows), part] = dot(weight, g_both[which, :, part]).astype(BF16)


def key_grad_kernel(tiles, first, last, where_ref, bias_ref, final_ref, *refs):
    refs = list(refs)
    count = len(tiles)
    take = lambda number: [refs.pop(0) for _ in range(number)]
    q_both, qt_ref, gt_ref, values_ref = take(4)
    if not first:
        (dq_in,) = take(1)
    if last:
        g_both, noisy_values_ref = take(2)
    keys_refs = take(count)
    dk_refs = take(count)
    if last:
        noisy_dv_ref, own_dq, next_dq, dq_ref = take(4)
    else:
        (dq_ref,) = take(1)
    rows = bias_ref.shape[-1]
    heads = values_ref.shape[1] // HEAD_DIM
    dq_ref[...] = jnp.zeros_like(dq_ref) if first else dq_in[...]
    for number, tile in enumerate(tiles):
        index, which = tile_place(where_ref, tile)
        for head in range(heads):
            part = lanes(head)
            keys = keys_refs[number][:, part]
            if tile is NOISY:
                values = noisy_values_ref[:, part]
            else:
                values = values_ref[value_rows(index, rows), part]
            raw = dot(keys, qt_ref[which, part, :]) * (SCALE * LOG2E)
            dweight = dot(values, gt_ref[which, part, :])
            shift = bias_ref[index] - final_ref[which, head : head + 1, :]
            delta = final_ref[which, heads + head : heads + head + 1, :]
            weights, dscores = [], []
            for block in range(rows // BLOCK):
                here = slice(block * BLOCK, (block + 1) * BLOCK)
                weight = jnp.exp2(raw[here] + shift[block : block + 1])
                weights.append(weight.astype(BF16))
                dscores.append((weight * (dweight[here] - delta)).astype(BF16))
            dscore = stacked(dscores)
            dk = dot(dscore, q_both[which, :, part])
            dk_refs[number][:, part] = dk.astype(dk_refs[number].dtype)
            dq_ref[which, part, :] += dot(keys.T, dscore)
            if tile is NOISY:
                noisy_dv_ref[:, part] = dot(stacked(weights), g_both[0, :, part]).astype(BF16)
    if last:
        for head in range(heads):
            part = lanes(head)
            own_dq[:, part] = dq_ref[0, part, :].T
            next_dq[:, part] = dq_ref[1, part, :].T.astype(BF16)


def finish_kernel(final_ref, acc_ref, acc_before_ref, dq_ref, dq_before_ref, out_ref, dq_out):
    heads = dq_ref.shape[1] // HEAD_DIM
    dq_out[...] = dq_ref[...] + dq_before_ref[...].astype(F32)
    for head in range(heads):
        part = lanes(head)
        row = lambda kind: final_ref[0, kind * heads + head : kind * heads + head + 1, :]
        output = acc_ref[part, :] * row(2) + acc_before_ref[part, :].astype(F32) * row(3)
        out_ref[:, part] = output.T.astype(BF16)


def call(body, name, outs, flops, *operands, unread=(), where=None, scratch=()):
    outs = [jax.ShapeDtypeStruct(shape, dtype) for shape, dtype in outs]
    sizes = [o.size * o.dtype.itemsize for o in (*operands, *outs)]
    scalars = () if where is None else (where,)
    operands = (*unread, *scalars, *operands)
    return pl.pallas_call(
        body,
        name=name,
        in_specs=[pl.BlockSpec(memory_space=pl.ANY)] * len(unread)
        + [pl.BlockSpec(memory_space=pltpu.SMEM)] * len(scalars)
        + [pl.BlockSpec(memory_space=pltpu.VMEM)] * (len(operands) - len(unread) - len(scalars)),
        out_specs=[pl.BlockSpec(memory_space=pltpu.VMEM)] * len(outs),
        out_shape=outs,
        scratch_shapes=scratch,
        compiler_params=pltpu.CompilerParams(vmem_limit_bytes=48 * 1024 * 1024),
        cost_estimate=pl.CostEstimate(
            flops=flops, bytes_accessed=sum(sizes), transcendentals=flops // 512
        ),
    )(*operands)


def row_sum(wide):
    folded = wide[:, lanes(0)]
    for head in range(1, wide.shape[1] // HEAD_DIM):
        folded = folded + wide[:, lanes(head)]
    return jnp.sum(folded.T, axis=0, keepdims=True)


def unit_kernel(full_width, raw_ref, totals_ref, gain_ref, out_ref):
    inverse = lax.rsqrt(totals_ref[...] / full_width + EPS).T
    out_ref[...] = (raw_ref[...].astype(F32) * inverse[:, :1] * gain_ref[...]).astype(BF16)


def inner_kernel(
    query_ref,
    noisy_ref,
    clean_ref,
    query_gain_ref,
    key_gain_ref,
    dq_ref,
    dkn_ref,
    dkc_ref,
    one_ref,
    other_ref,
    total_ref,
    inner_ref,
):
    total = dkc_ref[...] + one_ref[...].astype(F32) + other_ref[...].astype(F32)
    total_ref[...] = total
    inner_ref[...] = jnp.zeros_like(inner_ref)
    for index, (raw_ref, gain_ref, grad) in enumerate(
        (
            (clean_ref, key_gain_ref, total),
            (query_ref, query_gain_ref, dq_ref[...]),
            (noisy_ref, key_gain_ref, dkn_ref[...]),
        )
    ):
        inner_ref[index : index + 1, :] = row_sum(
            raw_ref[...].astype(F32) * (gain_ref[...] * (grad * SCALE))
        )


def unit_backward(values, inverse, term, inner, full_width):
    return (inverse[:, None] * term - values * (inverse**3 * inner / full_width)[:, None]).astype(
        BF16
    )


def local(
    queries,
    noisy_keys,
    noisy_values,
    clean_keys,
    clean_values,
    query_gain,
    key_gain,
    first_block,
    loss_mask,
    grad_output,
):
    row_count, local_width = queries.shape
    full_width = local_width * lax.axis_size("head")
    shard_count = lax.axis_size("seq")
    shard_index = lax.axis_index("seq")
    place = shard_index % RING
    block_count = row_count // BLOCK
    heads = local_width // HEAD_DIM
    wide = (row_count, local_width)
    turned = (local_width, row_count)
    both, both_turned = (2, *wide), (2, *turned)
    tile_flops = 2 * row_count * row_count * local_width

    values = ring_gather(clean_values)
    grad_masked = grad_output * loss_mask[:, None].astype(BF16)
    grad_next = shifted(grad_masked, -RING)
    first_next = shifted(first_block, -RING)

    query_raw = queries.astype(F32)
    noisy_raw = noisy_keys.astype(F32)
    clean_raw = clean_keys.astype(F32)
    totals = head_sum(
        jnp.concatenate(
            [
                jnp.sum(clean_raw * clean_raw, axis=1)[None],
                jnp.sum(query_raw * query_raw, axis=1)[None],
                jnp.sum(noisy_raw * noisy_raw, axis=1)[None],
                jnp.zeros((5, row_count), F32),
            ],
            axis=0,
        )
    )
    key_gain_row, query_gain_row = key_gain[None, :], query_gain[None, :]
    (clean_unit,) = call(
        partial(unit_kernel, float(full_width)),
        "unit",
        [(wide, BF16)],
        1 << 20,
        clean_keys,
        totals,
        key_gain_row,
    )
    first = (swapped(clean_unit, 0), swapped(clean_unit, 1))
    second = (swapped(first[1], 0), swapped(first[0], 1))
    third = (swapped(second[1], 0), swapped(second[0], 1))
    fourth = swapped(third[1], 0)

    inverse = lax.rsqrt(totals[:3] / full_width + EPS)
    clean_inverse, query_inverse, noisy_inverse = inverse[0], inverse[1], inverse[2]
    query_unit = (query_raw * query_inverse[:, None] * query_gain[None, :]).astype(BF16)
    noisy_unit = (noisy_raw * noisy_inverse[:, None] * key_gain[None, :]).astype(BF16)
    query_next = shifted(query_unit, -RING)

    def block_of(shard):
        return (shard * block_count + jnp.arange(row_count, dtype=jnp.int32) // BLOCK)[
            None, None, :
        ]

    def first_of(blocks):
        return jnp.repeat(blocks, BLOCK)[None, None, :]

    query_block = block_of(shard_index)
    next_block = block_of((shard_index + RING) % shard_count)
    places = jnp.arange(RING, dtype=jnp.int32)
    block_row = jnp.arange(block_count, dtype=jnp.int32)
    key_block = ((shard_index - place + places)[:, None] * block_count + block_row[None, :])[
        :, :, None
    ]
    seen = jnp.where(
        (places > place)[:, None, None],
        (key_block < next_block) & (key_block >= first_of(first_next)),
        (key_block < query_block) & (key_block >= first_of(first_block)),
    )
    own_block = (shard_index * block_count + block_row)[None, :, None]
    seen = jnp.concatenate([seen, own_block == query_block], axis=0)
    bias = jnp.where(seen, 0.0, HIDDEN).astype(F32)
    where = jnp.stack([place, place % 2]).astype(jnp.int32)

    early = [NOISY, OWN, *FIRST, *SECOND]
    late = [*THIRD, FOURTH]
    query_t, grad_t, q_both, g_both, stat, acc = call(
        partial(forward_kernel, early),
        "forward",
        [
            (both_turned, BF16),
            (both_turned, BF16),
            (both, BF16),
            (both, BF16),
            ((2 * len(early), heads, row_count), F32),
            ((len(early), *turned), F32),
        ],
        2 * len(early) * tile_flops,
        bias,
        query_unit,
        query_next,
        grad_masked,
        grad_next,
        noisy_values,
        values,
        noisy_unit,
        clean_unit,
        *first,
        *second,
        where=where,
    )
    stat_rows = (3 * heads, row_count)
    own_stat, next_stat, own_acc, next_acc = call(
        partial(forward_end_kernel, late, early),
        "forward",
        [(stat_rows, F32), (stat_rows, F32), (turned, F32), (turned, BF16)],
        4 * len(late) * tile_flops,
        bias,
        query_t,
        grad_t,
        stat,
        acc,
        values,
        *third,
        fourth,
        where=where,
    )
    before_stat = shifted(next_stat, RING)
    after_stat = shifted(own_stat, -RING)
    final, value_parts = call(
        partial(value_grad_kernel, [FOURTH, *THIRD, *SECOND, *FIRST, OWN]),
        "value_grad",
        [((2, 4 * heads, row_count), F32), ((RING * row_count, local_width), BF16)],
        2 * RING * tile_flops,
        bias,
        own_stat,
        next_stat,
        before_stat,
        after_stat,
        query_t,
        g_both,
        fourth,
        *third,
        *second,
        *first,
        clean_unit,
        where=where,
    )
    grad_clean_values = ring_scatter(value_parts)

    def key_grads(tiles, keys, types, carried):
        return call(
            partial(key_grad_kernel, tiles, not carried, False),
            "key_grad",
            [*[(wide, t) for t in types], (both_turned, F32)],
            4 * len(tiles) * tile_flops,
            bias,
            final,
            q_both,
            query_t,
            grad_t,
            values,
            *carried,
            *keys,
            where=where,
        )

    def joined(arrived, part):
        return (arrived.astype(F32) + part).astype(BF16)

    grad_fourth, grad_a3, grad_b3, *carried = key_grads(
        [FOURTH, *THIRD], (fourth, *third), [BF16, BF16, F32], ()
    )
    back_fourth = swapped(grad_fourth, 0)
    back_a3 = swapped(grad_a3, 0)
    grad_a2, grad_b2, *carried = key_grads(SECOND, second, [F32, F32], carried)
    back_b3 = swapped(joined(back_fourth, grad_b3), 1)
    grad_a1, grad_b1, *carried = key_grads(FIRST, first, [F32, F32], carried)
    back_b2 = swapped(joined(back_a3, grad_b2), 1)
    back_a2 = swapped(joined(back_b3, grad_a2), 0)
    back_a1 = swapped(joined(back_b2, grad_a1), 0)
    back_b1 = swapped(joined(back_a2, grad_b1), 1)
    own_key, noisy_key, noisy_value, own_dq, next_dq = call(
        partial(key_grad_kernel, [OWN, NOISY], False, True),
        "key_grad",
        [(wide, F32), (wide, F32), (wide, BF16), (wide, F32), (wide, BF16)],
        9 * tile_flops,
        bias,
        final,
        q_both,
        query_t,
        grad_t,
        values,
        *carried,
        g_both,
        noisy_values,
        clean_unit,
        noisy_unit,
        where=where,
        scratch=[pltpu.VMEM(both_turned, F32)],
    )
    acc_before = shifted(next_acc, RING)
    dq_before = shifted(next_dq, RING)
    attended, query_grad = call(
        finish_kernel,
        "finish",
        [(wide, BF16), (wide, F32)],
        1 << 20,
        final,
        own_acc,
        acc_before,
        own_dq,
        dq_before,
    )
    clean_grad, inner = call(
        inner_kernel,
        "inner",
        [(wide, F32), ((8, row_count), F32)],
        1 << 20,
        queries,
        noisy_keys,
        clean_keys,
        query_gain_row,
        key_gain_row,
        query_grad,
        noisy_key,
        own_key,
        back_a1,
        back_b1,
    )
    inner = head_sum(inner, (grad_clean_values,))

    query_term = query_gain[None, :] * (query_grad * SCALE)
    noisy_term = key_gain[None, :] * (noisy_key * SCALE)
    clean_term = key_gain[None, :] * (clean_grad * SCALE)
    grad_clean_keys = unit_backward(clean_raw, clean_inverse, clean_term, inner[0], full_width)
    grad_queries = unit_backward(query_raw, query_inverse, query_term, inner[1], full_width)
    grad_noisy_keys = unit_backward(noisy_raw, noisy_inverse, noisy_term, inner[2], full_width)
    return (
        attended,
        grad_queries,
        grad_noisy_keys,
        noisy_value,
        grad_clean_keys,
        grad_clean_values,
    )


def solution(mesh):
    spread = P("seq", "head")
    in_specs = (
        spread,
        spread,
        spread,
        spread,
        spread,
        P("head"),
        P("head"),
        P("seq"),
        P("seq"),
        spread,
    )
    return jax.shard_map(
        local, mesh=mesh, in_specs=in_specs, out_specs=(spread,) * 6, check_vma=False
    )
```
